256 devices in a mesh: row: 64 (over z, y, core), col: 4 (over x).
Axes of the slice: x: 4, y: 4, z: 8, core: 2. Of those that a mesh axis runs over, the one named last changes fastest.
Arguments:
- pair: bfloat16 [2048, 2048, 128], P(('row', 'col')), may hold values from -6 to 6
- pair_mask: int32 [2048, 2048], P(('row', 'col')), may hold values 0 or 1
- in_gain: float32 [128], replicated, may hold values from 0.25 to 1.75
- in_bias: float32 [128], replicated, may hold values from -3 to 3
- w_proj: bfloat16 [128, 512], replicated, may hold values from -0.5 to 0.5
- w_gate: bfloat16 [128, 128], replicated, may hold values from -0.5 to 0.5
- out_gain: float32 [128], replicated, may hold values from 0.25 to 1.75
- out_bias: float32 [128], replicated, may hold values from -3 to 3
- w_out: bfloat16 [128, 128], replicated, may hold values from -0.5 to 0.5
Outputs:
- update: bfloat16 [2048, 2048, 128], P(('row', 'col'))
The draws below stay inside these ranges and needn't reach their ends.
All inputs are finite; a program needn't handle non-finite values. No bound on the sum of `pair_mask` on one device may be relied on, other than what follows from the above.
Results may differ from the reference program's by a relative error of at most 0.0056.
Values may be sent and summed in bfloat16 or wider, within the bound.
No kernel may reach another device: no remote copies, remote signals or barrier semaphores. Data moves between devices by JAX's collectives and lax.ppermute only.
A program may use at most 320 MiB of HBM per device.

```python
import math
import jax
import jax.numpy as jnp
from jax import lax

C = 128
H = 128
TOKENS = 2048


def set_ends(result, stream_key, least, largest):
    place = [jax.random.randint(jax.random.fold_in(stream_key, axis), (), 0, length) for axis, length in enumerate(result.shape)]
    widest = result.shape.index(max(result.shape))
    beside = place[:widest] + [(place[widest] + 1) % result.shape[widest]] + place[widest + 1:]
    return result.at[tuple(place)].set(least).at[tuple(beside)].set(largest)


def shard_levels(own_key, extent, cuts, least, largest):
    loudness, own = 1.0, jax.random.fold_in(own_key, 6)
    for axis_at, parts in cuts:
        draws = jnp.exp(jax.random.uniform(jax.random.fold_in(own, axis_at), (parts,), jnp.float32, least / len(cuts), largest / len(cuts)))
        loudness = loudness * jnp.repeat(draws, extent[axis_at] // parts).reshape([-1 if axis == axis_at else 1 for axis in range(len(extent))])
    return loudness


def normal_values(own_key, shape, deviation, bound, cuts=(), kind=jnp.bfloat16):
    loudness = shard_levels(own_key, shape, cuts, -0.22, 0.18) if cuts else 1.0
    entries = jax.random.normal(own_key, shape, jnp.float32) * deviation * loudness
    return jnp.minimum(jnp.maximum(entries, -bound), bound).astype(kind)


def setup_inputs(seed: int = 0) -> dict:
    key_list = jax.random.split(jax.random.key(seed), 10)
    return {
        "pair": normal_values(key_list[0], (TOKENS, TOKENS, C), 1.0, 6.0, ((0, 256),)),
        "pair_mask": set_ends((jax.random.randint(key_list[1], (TOKENS, TOKENS), 0, 8) < 7).astype(jnp.int32), jax.random.fold_in(key_list[1], 1), 0, 1),
        "in_gain": jnp.clip(1.0 + 0.15 * jax.random.normal(key_list[2], (C,), jnp.float32), 0.25, 1.75),
        "in_bias": normal_values(key_list[3], (C,), 0.5, 3.0, (), jnp.float32),
        "w_proj": normal_values(key_list[4], (C, 4 * H), C ** -0.5, 0.5),
        "w_gate": normal_values(key_list[5], (C, C), C ** -0.5, 0.5),
        "out_gain": jnp.clip(1.0 + 0.15 * jax.random.normal(key_list[6], (H,), jnp.float32), 0.25, 1.75),
        "out_bias": normal_values(key_list[7], (H,), 0.5, 3.0, (), jnp.float32),
        "w_out": normal_values(key_list[8], (H, C), H ** -0.5, 0.5),
    }


def layer_norm(values, gain, bias):
    average = lax.optimization_barrier(jnp.mean(values, axis=-1, keepdims=True))
    centred = values - average
    spread = lax.optimization_barrier(jnp.mean(centred * centred, axis=-1, keepdims=True))
    return centred * lax.rsqrt(spread + 1e-05) * gain + bias

def reference(pair, pair_mask, in_gain, in_bias, w_proj, w_gate, out_gain, out_bias, w_out):
    total = pair.shape[0]
    channels = pair.shape[2]
    hidden_units = w_out.shape[0]
    block_rows = math.gcd(total, 64)
    block_count = total // block_rows

    def section_in(operands):
        pair_rows, mask_rows = operands
        normed = layer_norm(pair_rows.astype(jnp.float32), in_gain, in_bias).astype(jnp.bfloat16)
        proj = jnp.dot(normed.reshape(-1, channels), w_proj, preferred_element_type=jnp.float32)
        proj = proj.reshape(block_rows, total, 4 * hidden_units)
        keep_mask = mask_rows.astype(jnp.float32)[:, :, None]
        hu = hidden_units
        left_part = keep_mask * jax.nn.sigmoid(proj[..., :hu]) * proj[..., hu:2 * hu]
        right_part = keep_mask * jax.nn.sigmoid(proj[..., 2 * hu:3 * hu]) * proj[..., 3 * hu:]
        return (left_part.astype(jnp.bfloat16), right_part.astype(jnp.bfloat16))
    left_part, right_part = lax.map(section_in, (pair.reshape(block_count, block_rows, total, channels), pair_mask.reshape(block_count, block_rows, total)))
    left_part = left_part.reshape(total, total, hidden_units)
    right_part = right_part.reshape(total, total, hidden_units)
    channel_block = math.gcd(hidden_units, 4)

    def channel_product(first):
        left_slab = lax.dynamic_slice_in_dim(left_part, first, channel_block, 2).astype(jnp.float32)
        right_slab = lax.dynamic_slice_in_dim(right_part, first, channel_block, 2).astype(jnp.float32)
        return jnp.einsum('ikh,jkh->hij', left_slab, right_slab).astype(jnp.bfloat16)
    starts = (jnp.arange(hidden_units // channel_block) * channel_block).astype(jnp.int32)
    product = lax.map(channel_product, starts).reshape(hidden_units, total, total)
    product = jnp.transpose(product.reshape(hidden_units, block_count, block_rows, total), (1, 0, 2, 3))

    def section_out(operands):
        pair_rows, product_rows = operands
        values = jnp.transpose(product_rows.astype(jnp.float32), (1, 2, 0))
        post_norm = layer_norm(values, out_gain, out_bias).astype(jnp.bfloat16)
        projected = jnp.dot(post_norm.reshape(-1, hidden_units), w_out, preferred_element_type=jnp.float32)
        normed = layer_norm(pair_rows.astype(jnp.float32), in_gain, in_bias).astype(jnp.bfloat16)
        gate_value = jax.nn.sigmoid(jnp.dot(normed.reshape(-1, channels), w_gate, preferred_element_type=jnp.float32))
        return (gate_value * projected).astype(jnp.bfloat16).reshape(block_rows, total, channels)
    update = lax.map(section_out, (pair.reshape(block_count, block_rows, total, channels), product))
    return update.reshape(total, total, channels)
```

```python
import functools

import jax
import jax.numpy as jnp
from jax import lax
from jax.experimental import pallas as pl
from jax.experimental.pallas import tpu as pltpu
from jax.sharding import Mesh
from jax.sharding import PartitionSpec as P

NZ, NY, NCORE, NX = 8, 4, 2, 4
CHIPS = ("z", "y", "x")
ROWS = 8
LANES = 128
VMEM_LIMIT = 56 * 1024 * 1024


def rows_norm(x, gain, bias):
    average = jnp.mean(x, axis=-1, keepdims=True)
    centred = x - average
    spread = jnp.mean(centred * centred, axis=-1, keepdims=True)
    return centred * lax.rsqrt(spread + 1e-05) * gain + bias


def sigmoid(x):
    return 0.5 * jnp.tanh(0.5 * x) + 0.5


def enter_kernel(pair_ref, mask_ref, gain_ref, bias_ref, w_ref, left_ref, right_ref, normed_ref, lscr, rscr):
    hidden = w_ref.shape[0] // 4
    width = pair_ref.shape[1]
    gain = gain_ref[...]
    bias = bias_ref[...]
    keep = mask_ref[...].astype(jnp.float32)
    for i in range(ROWS):
        x = pair_ref[i].astype(jnp.float32)
        normed = rows_norm(x, gain, bias).astype(jnp.bfloat16)
        normed_ref[i] = normed
        for side, scr in ((0, lscr), (1, rscr)):
            proj = lax.dot_general(
                w_ref[2 * side * hidden : (2 * side + 2) * hidden],
                normed,
                (((1,), (1,)), ((), ())),
                preferred_element_type=jnp.float32,
            )
            value = sigmoid(proj[:hidden]) * proj[hidden:] * keep[i : i + 1]
            for t in range(width // LANES):
                scr[t, pl.ds(i, hidden, stride=ROWS), :] = value[:, t * LANES : (t + 1) * LANES]
    for t in range(width // LANES):
        lanes = pl.ds(t * LANES, LANES)
        left_ref[:, :, lanes] = lscr[t].reshape(hidden, ROWS, LANES).astype(jnp.bfloat16)
        right_ref[:, :, lanes] = rscr[t].reshape(hidden, ROWS, LANES).astype(jnp.bfloat16)


def enter(pair, mask, gain, bias, w_proj_t, width=256):
    rows, total, channels = pair.shape
    hidden = w_proj_t.shape[0] // 4
    whole = lambda *shape: pl.BlockSpec(shape, lambda k: (0,) * len(shape))
    side = jax.ShapeDtypeStruct((hidden, rows, total), jnp.bfloat16)
    side_spec = pl.BlockSpec((hidden, rows, width), lambda k: (0, 0, k))
    pair_spec = pl.BlockSpec((rows, width, channels), lambda k: (0, k, 0))
    return pl.pallas_call(
        enter_kernel,
        grid=(total // width,),
        in_specs=[
            pair_spec,
            pl.BlockSpec((rows, width), lambda k: (0, k)),
            whole(1, channels),
            whole(1, channels),
            whole(4 * hidden, channels),
        ],
        out_specs=[side_spec, side_spec, pair_spec],
        out_shape=[side, side, jax.ShapeDtypeStruct(pair.shape, jnp.bfloat16)],
        scratch_shapes=[pltpu.VMEM((width // LANES, hidden * rows, LANES), jnp.float32)] * 2,
        compiler_params=pltpu.CompilerParams(vmem_limit_bytes=VMEM_LIMIT),
        name="enter",
    )(pair, mask, gain, bias, w_proj_t)


def product_kernel(core_ref, a_ref, own_ref, other_ref, out_ref, b_scr, sems):
    @pl.when(pl.program_id(0) == 0)
    def _():
        core = core_ref[0]
        one = pltpu.make_async_copy(own_ref, b_scr.at[:, core], sems.at[0])
        two = pltpu.make_async_copy(other_ref, b_scr.at[:, 1 - core], sems.at[1])
        one.start()
        two.start()
        one.wait()
        two.wait()

    depth = a_ref.shape[1]
    out_ref[...] = lax.dot_general(
        a_ref[...],
        b_scr[...].reshape(-1, depth),
        (((1,), (1,)), ((), ())),
        preferred_element_type=jnp.float32,
    ).astype(jnp.bfloat16)


def product(core, a, own, other, height=128):
    m, depth = a.shape
    groups, part, _ = own.shape
    n = 2 * groups * part
    return pl.pallas_call(
        product_kernel,
        grid_spec=pltpu.PrefetchScalarGridSpec(
            num_scalar_prefetch=1,
            grid=(m // height,),
            in_specs=[
                pl.BlockSpec((height, depth), lambda i, c: (i, 0)),
                pl.BlockSpec(memory_space=pl.ANY),
                pl.BlockSpec(memory_space=pl.ANY),
            ],
            out_specs=pl.BlockSpec((height, n), lambda i, c: (i, 0)),
            scratch_shapes=[
                pltpu.VMEM((groups, 2, part, depth), jnp.bfloat16),
                pltpu.SemaphoreType.DMA((2,)),
            ],
        ),
        out_shape=jax.ShapeDtypeStruct((m, n), jnp.bfloat16),
        compiler_params=pltpu.CompilerParams(vmem_limit_bytes=VMEM_LIMIT),
        name="product",
    )(core, a, own, other)


def leave_kernel(prod_ref, normed_ref, gain_ref, bias_ref, w_out_ref, w_gate_ref, out_ref, scr):
    hidden, rows, width = prod_ref.shape
    values = prod_ref[...].astype(jnp.float32)
    average = jnp.sum(values, axis=0, keepdims=True) * (1.0 / hidden)
    centred = values - average
    spread = jnp.sum(centred * centred, axis=0, keepdims=True) * (1.0 / hidden)
    scaled = centred * lax.rsqrt(spread + 1e-05)
    for t in range(width // LANES):
        scr[t] = scaled[:, :, t * LANES : (t + 1) * LANES].reshape(hidden * rows, LANES)
    gain = gain_ref[...]
    bias = bias_ref[...]
    for i in range(rows):
        values = [scr[t, pl.ds(i, hidden, stride=rows), :] for t in range(width // LANES)]
        post = (jnp.concatenate(values, axis=1) * gain + bias).astype(jnp.bfloat16)
        projected = lax.dot_general(
            post, w_out_ref[...], (((0,), (0,)), ((), ())), preferred_element_type=jnp.float32
        )
        gate = jnp.dot(normed_ref[i], w_gate_ref[...], preferred_element_type=jnp.float32)
        out_ref[i] = (sigmoid(gate) * projected).astype(jnp.bfloat16)


def leave(prod, normed, gain, bias, w_out, w_gate, width=256):
    hidden, rows, total = prod.shape
    channels = normed.shape[2]
    whole = lambda *shape: pl.BlockSpec(shape, lambda k: (0,) * len(shape))
    pair_spec = pl.BlockSpec((rows, width, channels), lambda k: (0, k, 0))
    return pl.pallas_call(
        leave_kernel,
        grid=(total // width,),
        in_specs=[
            pl.BlockSpec((hidden, rows, width), lambda k: (0, 0, k)),
            pair_spec,
            whole(hidden, 1),
            whole(hidden, 1),
            whole(hidden, channels),
            whole(channels, channels),
        ],
        out_specs=pair_spec,
        out_shape=jax.ShapeDtypeStruct(normed.shape, jnp.bfloat16),
        scratch_shapes=[pltpu.VMEM((width // LANES, hidden * rows, LANES), jnp.float32)],
        compiler_params=pltpu.CompilerParams(vmem_limit_bytes=VMEM_LIMIT),
        name="leave",
    )(prod, normed, gain, bias, w_out, w_gate)


def shards(pair, pair_mask, in_gain, in_bias, w_proj, w_gate, out_gain, out_bias, w_out):
    rows, total, channels = pair.shape
    hidden = w_out.shape[0]
    left, right, normed = enter(
        pair, pair_mask, in_gain.reshape(1, -1), in_bias.reshape(1, -1), w_proj.T
    )
    exchange = functools.partial(lax.all_to_all, axis_name=CHIPS, split_axis=0, concat_axis=0, tiled=True)
    own = exchange(right)
    other = lax.ppermute(own, "core", [(0, 1), (1, 0)])
    a = exchange(left)
    groups = (NZ * NY, NX * rows, total)
    prod = product(
        lax.axis_index("core").reshape(1),
        a.reshape(hidden * rows, total),
        own.reshape(groups),
        other.reshape(groups),
    )
    back = exchange(prod.reshape(hidden, rows, total))
    return leave(
        back, normed, out_gain.reshape(-1, 1), out_bias.reshape(-1, 1), w_out, w_gate
    )


def solution(mesh):
    fine = Mesh(mesh.devices.reshape(NZ, NY, NCORE, NX), ("z", "y", "core", "x"))
    split = ("z", "y", "core", "x")
    return jax.shard_map(
        shards,
        mesh=fine,
        in_specs=(P(split), P(split), P(), P(), P(), P(), P(), P(), P()),
        out_specs=P(split),
        check_vma=False,
    )
```

```python
import functools

import jax
import jax.numpy as jnp
from jax import lax
from jax.experimental import pallas as pl
from jax.experimental.pallas import tpu as pltpu
from jax.sharding import Mesh
from jax.sharding import PartitionSpec as P

NZ, NY, NCORE, NX = 8, 4, 2, 4
CHIPS = ("z", "y", "x")
ROWS = 8
LANES = 128
VMEM_LIMIT = 56 * 1024 * 1024


def rows_norm(x, gain, bias):
    average = jnp.mean(x, axis=-1, keepdims=True)
    centred = x - average
    spread = jnp.mean(centred * centred, axis=-1, keepdims=True)
    return centred * lax.rsqrt(spread + 1e-05) * gain + bias


def sigmoid(x):
    return 0.5 * jnp.tanh(0.5 * x) + 0.5


def turned(w_ref, turned_ref):
    @pl.when(pl.program_id(0) == 0)
    def _():
        turned_ref[...] = w_ref[...].astype(jnp.float32).T.astype(jnp.bfloat16)

    return turned_ref


def gated(w_ref, normed, keep):
    hidden = w_ref.shape[0] // 2
    proj = lax.dot_general(
        w_ref[...], normed, (((1,), (1,)), ((), ())), preferred_element_type=jnp.float32
    )
    return sigmoid(proj[:hidden]) * proj[hidden:] * keep


def spread_rows(scr, i, value):
    for t in range(scr.shape[0]):
        part = value[:, t * LANES : (t + 1) * LANES]
        scr[t, pl.ds(i, value.shape[0], stride=ROWS), :] = part


def collect(scr, out_ref):
    hidden = out_ref.shape[0]
    for t in range(scr.shape[0]):
        block = scr[t].reshape(hidden, ROWS, LANES)
        out_ref[:, :, t * LANES : (t + 1) * LANES] = block.astype(jnp.bfloat16)


def enter_right_kernel(pair_ref, mask_ref, gain_ref, bias_ref, w_ref, right_ref, normed_ref, scr, w_scr):
    weights = turned(w_ref, w_scr)
    gain = gain_ref[...]
    bias = bias_ref[...]
    keep = mask_ref[...].astype(jnp.float32)
    for i in range(ROWS):
        normed = rows_norm(pair_ref[i].astype(jnp.float32), gain, bias).astype(jnp.bfloat16)
        normed_ref[i] = normed
        spread_rows(scr, i, gated(weights, normed, keep[i : i + 1]))
    collect(scr, right_ref)


def enter_left_kernel(normed_ref, mask_ref, w_ref, left_ref, scr, w_scr):
    weights = turned(w_ref, w_scr)
    keep = mask_ref[...].astype(jnp.float32)
    for i in range(ROWS):
        spread_rows(scr, i, gated(weights, normed_ref[i], keep[i : i + 1]))
    collect(scr, left_ref)


def whole(*shape):
    return pl.BlockSpec(shape, lambda *k: (0,) * len(shape))


def cost(flops, bytes_accessed, transcendentals=0):
    return pl.CostEstimate(
        flops=flops, bytes_accessed=bytes_accessed, transcendentals=transcendentals
    )


def enter(name, kernel, source, mask, weights, side_at, normed_too, first, columns, width=512):
    rows, total, channels = source.shape
    hidden = weights[-1].shape[1] // 4
    skip = first // width
    pair_spec = pl.BlockSpec((rows, width, channels), lambda k: (0, skip + k, 0))
    side_spec = pl.BlockSpec((hidden, rows, width), lambda k: (0, 0, k))
    side = jax.ShapeDtypeStruct((hidden, rows, columns), jnp.bfloat16)
    return pl.pallas_call(
        kernel,
        grid=(columns // width,),
        in_specs=[pair_spec, pl.BlockSpec((rows, width), lambda k: (0, skip + k))]
        + [whole(*w.shape) for w in weights[:-1]]
        + [pl.BlockSpec((channels, 2 * hidden), lambda k: (0, side_at))],
        out_specs=[side_spec, pair_spec] if normed_too else side_spec,
        out_shape=[side, jax.ShapeDtypeStruct(source.shape, jnp.bfloat16)] if normed_too else side,
        scratch_shapes=[
            pltpu.VMEM((width // LANES, hidden * rows, LANES), jnp.float32),
            pltpu.VMEM((2 * hidden, channels), jnp.bfloat16),
        ],
        compiler_params=pltpu.CompilerParams(vmem_limit_bytes=VMEM_LIMIT),
        cost_estimate=cost(4 * rows * columns * channels * hidden, 6 * rows * columns * channels, rows * columns * hidden),
        name=name,
    )(source, mask, *weights)


def product_kernel(own_steps, first_step, *refs):
    *a_refs, own_ref, other_ref, out_ref = refs

    def multiply(b_ref):
        total = None
        at = 0
        for a_ref in a_refs:
            depth = a_ref.shape[1]
            part = lax.dot_general(
                a_ref[...],
                b_ref[:, at : at + depth],
                (((1,), (1,)), ((), ())),
                preferred_element_type=jnp.float32,
            )
            total = part if total is None else total + part
            at += depth
        out_ref[...] = total.astype(jnp.bfloat16)

    first = pl.program_id(0) + first_step < own_steps
    pl.when(first)(lambda: multiply(own_ref))
    pl.when(jnp.logical_not(first))(lambda: multiply(other_ref))


def product(a_parts, own, other, first, columns, width=256):
    m = a_parts[0].shape[0]
    half, depth = own.shape
    steps, skip = half // width, first // width
    return pl.pallas_call(
        functools.partial(product_kernel, steps, skip),
        grid=(columns // width,),
        in_specs=[whole(*a.shape) for a in a_parts]
        + [
            pl.BlockSpec((width, depth), lambda k: (jnp.minimum(k + skip, steps - 1), 0)),
            pl.BlockSpec((width, depth), lambda k: (jnp.maximum(k + skip - steps, 0), 0)),
        ],
        out_specs=pl.BlockSpec((m, width), lambda k: (0, k)),
        out_shape=jax.ShapeDtypeStruct((m, columns), jnp.bfloat16),
        compiler_params=pltpu.CompilerParams(vmem_limit_bytes=VMEM_LIMIT),
        cost_estimate=cost(2 * m * depth * columns, 2 * m * depth + 2 * columns * depth + 2 * m * columns),
        name="product",
    )(*a_parts, own, other)


def leave_kernel(core_ref, prod_ref, normed_ref, gain_ref, bias_ref, w_out_ref, w_gate_ref, *refs):
    out_ref, scr = refs[-2:]
    hidden, rows, width = prod_ref.shape
    values = prod_ref[...].astype(jnp.float32)
    average = jnp.sum(values, axis=0, keepdims=True) * (1.0 / hidden)
    centred = values - average
    spread = jnp.sum(centred * centred, axis=0, keepdims=True) * (1.0 / hidden)
    scaled = centred * lax.rsqrt(spread + 1e-05)
    for t in range(width // LANES):
        scr[t] = scaled[:, :, t * LANES : (t + 1) * LANES].reshape(hidden * rows, LANES)
    gain = gain_ref[...]
    bias = bias_ref[...]
    for i in range(rows):
        values = [scr[t, pl.ds(i, hidden, stride=rows), :] for t in range(width // LANES)]
        post = (jnp.concatenate(values, axis=1) * gain + bias).astype(jnp.bfloat16)
        projected = lax.dot_general(
            post, w_out_ref[...], (((0,), (0,)), ((), ())), preferred_element_type=jnp.float32
        )
        normed = normed_ref[i].reshape(width, -1)
        gate = jnp.dot(normed, w_gate_ref[...], preferred_element_type=jnp.float32)
        out_ref[i] = (sigmoid(gate) * projected).astype(jnp.bfloat16).reshape(out_ref.shape[1:])


def leave(core, prod, normed, gain, bias, w_out, w_gate, first, before=None, width=512):
    hidden, rows, columns = prod.shape
    _, groups, _, part, channels = normed.shape
    count = width // part
    steps, skip = groups // count, first // width
    more = [] if before is None else [before]
    pair_spec = pl.BlockSpec(
        (rows, count, None, part, channels),
        lambda k, c: (0, lax.rem(k + skip, steps), jnp.where(k + skip < steps, c[0], 1 - c[0]), 0, 0),
    )
    return pl.pallas_call(
        leave_kernel,
        grid_spec=pltpu.PrefetchScalarGridSpec(
            num_scalar_prefetch=1,
            grid=(columns // width,),
            in_specs=[
                pl.BlockSpec((hidden, rows, width), lambda k, c: (0, 0, k)),
                pair_spec,
                whole(hidden, 1),
                whole(hidden, 1),
                whole(hidden, channels),
                whole(channels, channels),
            ]
            + [pl.BlockSpec(memory_space=pl.ANY)] * len(more),
            out_specs=pair_spec,
            scratch_shapes=[pltpu.VMEM((width // LANES, hidden * rows, LANES), jnp.float32)],
        ),
        out_shape=jax.ShapeDtypeStruct(normed.shape, jnp.bfloat16),
        input_output_aliases={7: 0} if more else {},
        compiler_params=pltpu.CompilerParams(vmem_limit_bytes=VMEM_LIMIT),
        cost_estimate=cost(4 * prod.size * channels, 6 * prod.size, prod.size),
        name="leave",
    )(core, prod, normed, gain, bias, w_out, w_gate, *more)


def shards(pair, pair_mask, in_gain, in_bias, w_proj, w_gate, out_gain, out_bias, w_out):
    rows, total, channels = pair.shape
    hidden = w_out.shape[0]
    right, normed = enter(
        "enter_right",
        enter_right_kernel,
        pair,
        pair_mask,
        (in_gain.reshape(1, -1), in_bias.reshape(1, -1), w_proj),
        1,
        True,
        0,
        total,
    )
    enter_left = functools.partial(
        enter, "enter_left", enter_left_kernel, normed, pair_mask, (w_proj,), 0, False
    )
    exchange = functools.partial(lax.all_to_all, axis_name=CHIPS, split_axis=0, concat_axis=0, tiled=True)
    matrix = (hidden * rows, -1)
    own = exchange(right)
    other = lax.ppermute(own, "core", [(0, 1), (1, 0)])
    a_parts = [exchange(enter_left(0, total)).reshape(matrix)]
    core = lax.axis_index("core").reshape(1)
    normed = normed.reshape(rows, NZ * NY, NCORE, NX * rows, channels)
    vectors = (out_gain.reshape(-1, 1), out_bias.reshape(-1, 1), w_out, w_gate)
    own, other = own.reshape(matrix), other.reshape(matrix)
    rest = product(a_parts, own, other, 0, total).reshape(hidden, rows, -1)
    out = leave(core, exchange(rest), normed, *vectors, 0)
    return out.reshape(pair.shape)


def solution(mesh):
    fine = Mesh(mesh.devices.reshape(NZ, NY, NCORE, NX), ("z", "y", "core", "x"))
    split = ("z", "y", "core", "x")
    return jax.shard_map(
        shards,
        mesh=fine,
        in_specs=(P(split), P(split), P(), P(), P(), P(), P(), P(), P()),
        out_specs=P(split),
        check_vma=False,
    )
```

```python
import functools

import jax
import jax.numpy as jnp
from jax import lax
from jax.experimental import pallas as pl
from jax.experimental.pallas import tpu as pltpu
from jax.sharding import Mesh
from jax.sharding import PartitionSpec as P

NZ, NY, NCORE, NX = 8, 4, 2, 4
CHIPS = ("z", "y", "x")
ROWS = 8
LANES = 128
MIB = 1024 * 1024
VMEM_LIMIT = 56 * MIB


def rows_norm(x, gain, bias):
    average = jnp.mean(x, axis=-1, keepdims=True)
    centred = x - average
    spread = jnp.mean(centred * centred, axis=-1, keepdims=True)
    return centred * lax.rsqrt(spread + 1e-05) * gain + bias


def sigmoid(x):
    return 0.5 * jnp.tanh(0.5 * x) + 0.5


def turned(w_ref, turned_ref):
    @pl.when(pl.program_id(0) == 0)
    def _():
        turned_ref[...] = w_ref[...].astype(jnp.float32).T.astype(jnp.bfloat16)

    return turned_ref


def gated(w_ref, normed, keep):
    hidden = w_ref.shape[0] // 2
    proj = lax.dot_general(
        w_ref[...], normed, (((1,), (1,)), ((), ())), preferred_element_type=jnp.float32
    )
    return sigmoid(proj[:hidden]) * proj[hidden:] * keep


def spread_rows(scr, i, value):
    for t in range(scr.shape[0]):
        part = value[:, t * LANES : (t + 1) * LANES]
        scr[t, pl.ds(i, value.shape[0], stride=ROWS), :] = part


def collect(scr, out_ref):
    hidden = out_ref.shape[0]
    for t in range(scr.shape[0]):
        block = scr[t].reshape(hidden, ROWS, LANES)
        out_ref[:, :, t * LANES : (t + 1) * LANES] = block.astype(jnp.bfloat16)


def enter_kernel(pair_ref, mask_ref, gain_ref, bias_ref, w_ref, side_ref, *refs):
    *normed_refs, scr, w_scr = refs
    weights = turned(w_ref, w_scr)
    keep = mask_ref[...].astype(jnp.float32)
    rows, width, channels = pair_ref.shape
    values = pair_ref[...].reshape(rows * width, channels).astype(jnp.float32)
    normed = rows_norm(values, gain_ref[...], bias_ref[...]).astype(jnp.bfloat16)
    for i in range(rows):
        part = normed[i * width : (i + 1) * width]
        for normed_ref in normed_refs:
            normed_ref[i] = part
        spread_rows(scr, i, gated(weights, part, keep[i : i + 1]))
    collect(scr, side_ref)


def whole(*shape):
    return pl.BlockSpec(shape, lambda *k: (0,) * len(shape))


def cost(flops, bytes_accessed, transcendentals=0):
    return pl.CostEstimate(
        flops=flops, bytes_accessed=bytes_accessed, transcendentals=transcendentals
    )


def enter(name, pair, mask, gain, bias, w_proj, side_at, normed_too, width=512):
    rows, total, channels = pair.shape
    hidden = w_proj.shape[1] // 4
    pair_spec = pl.BlockSpec((rows, width, channels), lambda k: (0, k, 0))
    side = jax.ShapeDtypeStruct((hidden, rows, total), jnp.bfloat16)
    return pl.pallas_call(
        enter_kernel,
        grid=(total // width,),
        in_specs=[
            pair_spec,
            pl.BlockSpec((rows, width), lambda k: (0, k)),
            whole(1, channels),
            whole(1, channels),
            pl.BlockSpec((channels, 2 * hidden), lambda k: (0, side_at)),
        ],
        out_specs=[pl.BlockSpec((hidden, rows, width), lambda k: (0, 0, k))] + [pair_spec] * normed_too,
        out_shape=[side] + [jax.ShapeDtypeStruct(pair.shape, jnp.bfloat16)] * normed_too,
        scratch_shapes=[
            pltpu.VMEM((width // LANES, hidden * rows, LANES), jnp.float32),
            pltpu.VMEM((2 * hidden, channels), jnp.bfloat16),
        ],
        compiler_params=pltpu.CompilerParams(vmem_limit_bytes=VMEM_LIMIT),
        cost_estimate=cost(4 * pair.size * hidden, 6 * pair.size, pair.size),
        name=name,
    )(pair, mask, gain, bias, w_proj)


def product_kernel(own_steps, a_ref, own_ref, other_ref, out_ref):
    def multiply(b_ref):
        out_ref[...] = lax.dot_general(
            a_ref[...],
            b_ref[...],
            (((1,), (1,)), ((), ())),
            preferred_element_type=jnp.float32,
        ).astype(jnp.bfloat16)

    step = pl.program_id(0)
    pl.when(step < own_steps)(lambda: multiply(own_ref))
    pl.when(step >= own_steps)(lambda: multiply(other_ref))


def product(a, own, other, width=512):
    m, depth = a.shape
    half = own.shape[0]
    steps = half // width
    return pl.pallas_call(
        functools.partial(product_kernel, steps),
        grid=(2 * steps,),
        in_specs=[
            whole(m, depth),
            pl.BlockSpec((width, depth), lambda k: (jnp.minimum(k, steps - 1), 0)),
            pl.BlockSpec((width, depth), lambda k: (jnp.maximum(k - steps, 0), 0)),
        ],
        out_specs=pl.BlockSpec((m, width), lambda k: (0, k)),
        out_shape=jax.ShapeDtypeStruct((m, 2 * half), jnp.bfloat16),
        compiler_params=pltpu.CompilerParams(vmem_limit_bytes=VMEM_LIMIT),
        cost_estimate=cost(4 * m * depth * half, 2 * (m * depth + 2 * half * depth + 2 * m * half)),
        name="product",
    )(a, own, other)


def leave_kernel(core_ref, prod_ref, normed_ref, gain_ref, bias_ref, w_ref, out_ref, scr):
    hidden, rows, width = prod_ref.shape
    channels = normed_ref.shape[-1]
    values = prod_ref[...].astype(jnp.float32)
    average = jnp.sum(values, axis=0, keepdims=True) * (1.0 / hidden)
    centred = values - average
    spread = jnp.sum(centred * centred, axis=0, keepdims=True) * (1.0 / hidden)
    scaled = centred * lax.rsqrt(spread + 1e-05)
    for t in range(width // LANES):
        scr[t] = scaled[:, :, t * LANES : (t + 1) * LANES].reshape(hidden * rows, LANES)
    gain = gain_ref[...]
    bias = bias_ref[...]
    for i in range(rows):
        post = jnp.concatenate(
            [
                (scr[t, pl.ds(i, hidden, stride=rows), :].T * gain + bias).astype(jnp.bfloat16)
                for t in range(width // LANES)
            ],
            axis=0,
        )
        normed = normed_ref[i].reshape(width, channels)
        result = jnp.dot(
            jnp.concatenate([post, normed], axis=1), w_ref[...], preferred_element_type=jnp.float32
        )
        update = sigmoid(result[:, channels:]) * result[:, :channels]
        out_ref[i] = update.astype(jnp.bfloat16).reshape(out_ref.shape[1:])


def leave(core, prod, normed, gain, bias, w, width=512):
    hidden, rows, columns = prod.shape
    _, groups, _, part, channels = normed.shape
    count = width // part
    steps = groups // count
    pair_spec = pl.BlockSpec(
        (rows, count, None, part, channels),
        lambda k, c: (0, lax.rem(k, steps), jnp.where(k < steps, c[0], 1 - c[0]), 0, 0),
    )
    return pl.pallas_call(
        leave_kernel,
        grid_spec=pltpu.PrefetchScalarGridSpec(
            num_scalar_prefetch=1,
            grid=(columns // width,),
            in_specs=[
                pl.BlockSpec((hidden, rows, width), lambda k, c: (0, 0, k)),
                pair_spec,
                whole(1, hidden),
                whole(1, hidden),
                whole(*w.shape),
            ],
            out_specs=pair_spec,
            scratch_shapes=[pltpu.VMEM((width // LANES, hidden * rows, LANES), jnp.float32)],
        ),
        out_shape=jax.ShapeDtypeStruct(normed.shape, jnp.bfloat16),
        compiler_params=pltpu.CompilerParams(vmem_limit_bytes=VMEM_LIMIT),
        cost_estimate=cost(4 * prod.size * channels, 6 * prod.size, prod.size),
        name="leave",
    )(core, prod, normed, gain, bias, w)


def shards(pair, pair_mask, in_gain, in_bias, w_proj, w_gate, out_gain, out_bias, w_out):
    rows, total, channels = pair.shape
    hidden = w_out.shape[0]
    given = (pair, pair_mask, in_gain.reshape(1, -1), in_bias.reshape(1, -1), w_proj)
    (right,) = enter("enter_right", *given, 1, False)
    left, normed = enter("enter_left", *given, 0, True)
    exchange = functools.partial(lax.all_to_all, axis_name=CHIPS, split_axis=0, concat_axis=0, tiled=True)
    matrix = (hidden * rows, total)
    own = exchange(right)
    other = lax.ppermute(own, "core", [(0, 1), (1, 0)])
    prod = product(exchange(left).reshape(matrix), own.reshape(matrix), other.reshape(matrix))
    back = exchange(prod.reshape(hidden, rows, total))
    w_both = jnp.zeros((hidden + channels, 2 * channels), jnp.bfloat16)
    w_both = w_both.at[:hidden, :channels].set(w_out).at[hidden:, channels:].set(w_gate)
    out = leave(
        lax.axis_index("core").reshape(1),
        back,
        normed.reshape(rows, NZ * NY, NCORE, NX * rows, channels),
        out_gain.reshape(1, -1),
        out_bias.reshape(1, -1),
        w_both,
    )
    return out.reshape(pair.shape)


def solution(mesh):
    fine = Mesh(mesh.devices.reshape(NZ, NY, NCORE, NX), ("z", "y", "core", "x"))
    split = ("z", "y", "core", "x")
    return jax.shard_map(
        shards,
        mesh=fine,
        in_specs=(P(split), P(split), P(), P(), P(), P(), P(), P(), P()),
        out_specs=P(split),
        check_vma=False,
    )
```

```python
import functools

import jax
import jax.numpy as jnp
from jax import lax
from jax.experimental import pallas as pl
from jax.experimental.pallas import tpu as pltpu
from jax.sharding import Mesh
from jax.sharding import PartitionSpec as P

NZ, NY, NCORE, NX = 8, 4, 2, 4
CHIPS = ("z", "y", "x")
ROWS = 8
LANES = 128
MIB = 1024 * 1024
VMEM_LIMIT = 56 * MIB


def rows_norm(x, gain, bias):
    average = jnp.mean(x, axis=-1, keepdims=True)
    centred = x - average
    spread = jnp.mean(centred * centred, axis=-1, keepdims=True)
    return centred * lax.rsqrt(spread + 1e-05) * gain + bias


def gate_by(half_gate, half_value):
    return (jnp.tanh(half_gate) + 1.0) * half_value


def turned(w_ref, turned_ref):
    @pl.when(pl.program_id(0) == 0)
    def _():
        turned_ref[...] = (w_ref[...].astype(jnp.float32).T * 0.5).astype(jnp.bfloat16)

    return turned_ref


def gated(w_ref, normed, keep):
    hidden = w_ref.shape[0] // 2
    proj = lax.dot_general(
        w_ref[...], normed, (((1,), (1,)), ((), ())), preferred_element_type=jnp.float32
    )
    return gate_by(proj[:hidden], proj[hidden:] * keep)


def spread_rows(scr, i, value):
    for t in range(scr.shape[0]):
        part = value[:, t * LANES : (t + 1) * LANES]
        scr[t, pl.ds(i, value.shape[0], stride=ROWS), :] = part


def collect(scr, out_ref):
    hidden = out_ref.shape[0]
    for t in range(scr.shape[0]):
        block = scr[t].reshape(hidden, ROWS, LANES)
        out_ref[:, :, t * LANES : (t + 1) * LANES] = block.astype(jnp.bfloat16)


def enter_kernel(pair_ref, mask_ref, gain_ref, bias_ref, w_ref, side_ref, *refs):
    *normed_refs, scr, w_scr = refs
    weights = turned(w_ref, w_scr)
    keep = mask_ref[...].astype(jnp.float32)
    rows, width, channels = pair_ref.shape
    values = pair_ref[...].reshape(rows * width, channels).astype(jnp.float32)
    normed = rows_norm(values, gain_ref[...], bias_ref[...]).astype(jnp.bfloat16)
    for i in range(rows):
        part = normed[i * width : (i + 1) * width]
        for normed_ref in normed_refs:
            normed_ref[i] = part
        spread_rows(scr, i, gated(weights, part, keep[i : i + 1]))
    collect(scr, side_ref)


def whole(*shape):
    return pl.BlockSpec(shape, lambda *k: (0,) * len(shape))


def cost(flops, bytes_accessed, transcendentals=0):
    return pl.CostEstimate(
        flops=flops, bytes_accessed=bytes_accessed, transcendentals=transcendentals
    )


def enter(name, pair, mask, gain, bias, w_proj, side_at, normed_too, width=512):
    rows, total, channels = pair.shape
    hidden = w_proj.shape[1] // 4
    pair_spec = pl.BlockSpec((rows, width, channels), lambda k: (0, k, 0))
    side = jax.ShapeDtypeStruct((hidden, rows, total), jnp.bfloat16)
    return pl.pallas_call(
        enter_kernel,
        grid=(total // width,),
        in_specs=[
            pair_spec,
            pl.BlockSpec((rows, width), lambda k: (0, k)),
            whole(1, channels),
            whole(1, channels),
            pl.BlockSpec((channels, 2 * hidden), lambda k: (0, side_at)),
        ],
        out_specs=[pl.BlockSpec((hidden, rows, width), lambda k: (0, 0, k))] + [pair_spec] * normed_too,
        out_shape=[side] + [jax.ShapeDtypeStruct(pair.shape, jnp.bfloat16)] * normed_too,
        scratch_shapes=[
            pltpu.VMEM((width // LANES, hidden * rows, LANES), jnp.float32),
            pltpu.VMEM((2 * hidden, channels), jnp.bfloat16),
        ],
        compiler_params=pltpu.CompilerParams(vmem_limit_bytes=VMEM_LIMIT),
        cost_estimate=cost(4 * pair.size * hidden, 6 * pair.size, pair.size),
        name=name,
    )(pair, mask, gain, bias, w_proj)


def product_kernel(own_steps, a_ref, own_ref, other_ref, out_ref):
    def multiply(b_ref):
        out_ref[...] = lax.dot_general(
            a_ref[...],
            b_ref[...],
            (((1,), (1,)), ((), ())),
            preferred_element_type=jnp.float32,
        ).astype(jnp.bfloat16)

    step = pl.program_id(0)
    pl.when(step < own_steps)(lambda: multiply(own_ref))
    pl.when(step >= own_steps)(lambda: multiply(other_ref))


def product(a, own, other, width=512):
    m, depth = a.shape
    half = own.shape[0]
    steps = half // width
    return pl.pallas_call(
        functools.partial(product_kernel, steps),
        grid=(2 * steps,),
        in_specs=[
            whole(m, depth),
            pl.BlockSpec((width, depth), lambda k: (jnp.minimum(k, steps - 1), 0)),
            pl.BlockSpec((width, depth), lambda k: (jnp.maximum(k - steps, 0), 0)),
        ],
        out_specs=pl.BlockSpec((m, width), lambda k: (0, k)),
        out_shape=jax.ShapeDtypeStruct((m, 2 * half), jnp.bfloat16),
        compiler_params=pltpu.CompilerParams(vmem_limit_bytes=VMEM_LIMIT),
        cost_estimate=cost(4 * m * depth * half, 2 * (m * depth + 2 * half * depth + 2 * m * half)),
        name="product",
    )(a, own, other)


def leave_kernel(core_ref, prod_ref, normed_ref, gain_ref, bias_ref, w_ref, out_ref, scr):
    hidden, rows, width = prod_ref.shape
    channels = normed_ref.shape[-1]
    values = prod_ref[...].astype(jnp.float32)
    average = jnp.sum(values, axis=0, keepdims=True) * (1.0 / hidden)
    centred = values - average
    spread = jnp.sum(centred * centred, axis=0, keepdims=True) * (1.0 / hidden)
    scaled = centred * lax.rsqrt(spread + 1e-05)
    for t in range(width // LANES):
        scr[t] = scaled[:, :, t * LANES : (t + 1) * LANES].reshape(hidden * rows, LANES)
    gain = gain_ref[...]
    bias = bias_ref[...]
    for i in range(rows):
        post = jnp.concatenate(
            [
                (scr[t, pl.ds(i, hidden, stride=rows), :].T * gain + bias).astype(jnp.bfloat16)
                for t in range(width // LANES)
            ],
            axis=0,
        )
        normed = normed_ref[i].reshape(width, channels)
        result = jnp.dot(
            jnp.concatenate([post, normed], axis=1), w_ref[...], preferred_element_type=jnp.float32
        )
        update = gate_by(result[:, channels:], result[:, :channels])
        out_ref[i] = update.astype(jnp.bfloat16).reshape(out_ref.shape[1:])


def leave(core, prod, normed, gain, bias, w, width=512):
    hidden, rows, columns = prod.shape
    _, groups, _, part, channels = normed.shape
    count = width // part
    steps = groups // count
    pair_spec = pl.BlockSpec(
        (rows, count, None, part, channels),
        lambda k, c: (0, lax.rem(k, steps), jnp.where(k < steps, c[0], 1 - c[0]), 0, 0),
    )
    return pl.pallas_call(
        leave_kernel,
        grid_spec=pltpu.PrefetchScalarGridSpec(
            num_scalar_prefetch=1,
            grid=(columns // width,),
            in_specs=[
                pl.BlockSpec((hidden, rows, width), lambda k, c: (0, 0, k)),
                pair_spec,
                whole(1, hidden),
                whole(1, hidden),
                whole(*w.shape),
            ],
            out_specs=pair_spec,
            scratch_shapes=[pltpu.VMEM((width // LANES, hidden * rows, LANES), jnp.float32)],
        ),
        out_shape=jax.ShapeDtypeStruct(normed.shape, jnp.bfloat16),
        compiler_params=pltpu.CompilerParams(vmem_limit_bytes=VMEM_LIMIT),
        cost_estimate=cost(4 * prod.size * channels, 6 * prod.size, prod.size),
        name="leave",
    )(core, prod, normed, gain, bias, w)


def shards(pair, pair_mask, in_gain, in_bias, w_proj, w_gate, out_gain, out_bias, w_out):
    rows, total, channels = pair.shape
    hidden = w_out.shape[0]
    given = (pair, pair_mask, in_gain.reshape(1, -1), in_bias.reshape(1, -1), w_proj)
    (right,) = enter("enter_right", *given, 1, False)
    left, normed = enter("enter_left", *given, 0, True)
    exchange = functools.partial(lax.all_to_all, axis_name=CHIPS, split_axis=0, concat_axis=0, tiled=True)
    matrix = (hidden * rows, total)
    own = exchange(right)
    other = lax.ppermute(own, "core", [(0, 1), (1, 0)])
    prod = product(exchange(left).reshape(matrix), own.reshape(matrix), other.reshape(matrix))
    back = exchange(prod.reshape(hidden, rows, total))
    w_both = jnp.zeros((hidden + channels, 2 * channels), jnp.bfloat16)
    w_both = w_both.at[:hidden, :channels].set(w_out * 0.5).at[hidden:, channels:].set(w_gate * 0.5)
    out = leave(
        lax.axis_index("core").reshape(1),
        back,
        normed.reshape(rows, NZ * NY, NCORE, NX * rows, channels),
        out_gain.reshape(1, -1),
        out_bias.reshape(1, -1),
        w_both,
    )
    return out.reshape(pair.shape)


def solution(mesh):
    fine = Mesh(mesh.devices.reshape(NZ, NY, NCORE, NX), ("z", "y", "core", "x"))
    split = ("z", "y", "core", "x")
    return jax.shard_map(
        shards,
        mesh=fine,
        in_specs=(P(split), P(split), P(), P(), P(), P(), P(), P(), P()),
        out_specs=P(split),
        check_vma=False,
    )
```

```python
import functools

import jax
import jax.numpy as jnp
from jax import lax
from jax.experimental import pallas as pl
from jax.experimental.pallas import tpu as pltpu
from jax.sharding import Mesh
from jax.sharding import PartitionSpec as P

NZ, NY, NCORE, NX = 8, 4, 2, 4
CHIPS = ("z", "y", "x")
ROWS = 8
LANES = 128
MIB = 1024 * 1024
VMEM_LIMIT = 56 * MIB


def rows_norm(values, gain, bias):
    channels = values.shape[-1]
    share = jnp.full((channels, channels), 1.0 / channels, jnp.bfloat16)
    average = jnp.dot(values, share, preferred_element_type=jnp.float32)
    centred = values.astype(jnp.float32) - average
    spread = jnp.mean(centred * centred, axis=-1, keepdims=True)
    return centred * lax.rsqrt(spread + 1e-05) * gain + bias


def gate_by(half_gate, half_value):
    return (jnp.tanh(half_gate) + 1.0) * half_value


def turned(w_ref, turned_ref):
    @pl.when(pl.program_id(0) == 0)
    def _():
        turned_ref[...] = (w_ref[...].astype(jnp.float32).T * 0.5).astype(jnp.bfloat16)

    return turned_ref


def gated(w_ref, normed, keep):
    hidden = w_ref.shape[0] // 2
    proj = lax.dot_general(
        w_ref[...], normed, (((1,), (1,)), ((), ())), preferred_element_type=jnp.float32
    )
    return gate_by(proj[:hidden], proj[hidden:] * keep)


def spread_rows(scr, i, value):
    for t in range(scr.shape[0]):
        part = value[:, t * LANES : (t + 1) * LANES]
        scr[t, pl.ds(i, value.shape[0], stride=ROWS), :] = part


def collect(scr, out_ref):
    hidden = out_ref.shape[0]
    for t in range(scr.shape[0]):
        block = scr[t].reshape(hidden, ROWS, LANES)
        out_ref[:, :, t * LANES : (t + 1) * LANES] = block.astype(jnp.bfloat16)


def enter_kernel(pair_ref, mask_ref, gain_ref, bias_ref, w_ref, side_ref, *refs):
    *normed_refs, scr, w_scr = refs
    weights = turned(w_ref, w_scr)
    keep = mask_ref[...].astype(jnp.float32)
    rows, width, channels = pair_ref.shape
    values = pair_ref[...].reshape(rows * width, channels)
    normed = rows_norm(values, gain_ref[...], bias_ref[...]).astype(jnp.bfloat16)
    for i in range(rows):
        part = normed[i * width : (i + 1) * width]
        for normed_ref in normed_refs:
            normed_ref[i] = part
        spread_rows(scr, i, gated(weights, part, keep[i : i + 1]))
    collect(scr, side_ref)


def whole(*shape):
    return pl.BlockSpec(shape, lambda *k: (0,) * len(shape))


def cost(flops, bytes_accessed, transcendentals=0):
    return pl.CostEstimate(
        flops=flops, bytes_accessed=bytes_accessed, transcendentals=transcendentals
    )


def enter(name, pair, mask, gain, bias, w_proj, side_at, normed_too, width=512):
    rows, total, channels = pair.shape
    hidden = w_proj.shape[1] // 4
    pair_spec = pl.BlockSpec((rows, width, channels), lambda k: (0, k, 0))
    side = jax.ShapeDtypeStruct((hidden, rows, total), jnp.bfloat16)
    return pl.pallas_call(
        enter_kernel,
        grid=(total // width,),
        in_specs=[
            pair_spec,
            pl.BlockSpec((rows, width), lambda k: (0, k)),
            whole(1, channels),
            whole(1, channels),
            pl.BlockSpec((channels, 2 * hidden), lambda k: (0, side_at)),
        ],
        out_specs=[pl.BlockSpec((hidden, rows, width), lambda k: (0, 0, k))] + [pair_spec] * normed_too,
        out_shape=[side] + [jax.ShapeDtypeStruct(pair.shape, jnp.bfloat16)] * normed_too,
        scratch_shapes=[
            pltpu.VMEM((width // LANES, hidden * rows, LANES), jnp.float32),
            pltpu.VMEM((2 * hidden, channels), jnp.bfloat16),
        ],
        compiler_params=pltpu.CompilerParams(vmem_limit_bytes=VMEM_LIMIT),
        cost_estimate=cost(4 * pair.size * hidden, 6 * pair.size, pair.size),
        name=name,
    )(pair, mask, gain, bias, w_proj)


def product_kernel(own_steps, a_ref, own_ref, other_ref, out_ref):
    def multiply(b_ref):
        out_ref[...] = lax.dot_general(
            a_ref[...],
            b_ref[...],
            (((1,), (1,)), ((), ())),
            preferred_element_type=jnp.float32,
        ).astype(jnp.bfloat16)

    step = pl.program_id(0)
    pl.when(step < own_steps)(lambda: multiply(own_ref))
    pl.when(step >= own_steps)(lambda: multiply(other_ref))


def product(a, own, other, width=512):
    m, depth = a.shape
    half = own.shape[0]
    steps = half // width
    return pl.pallas_call(
        functools.partial(product_kernel, steps),
        grid=(2 * steps,),
        in_specs=[
            whole(m, depth),
            pl.BlockSpec((width, depth), lambda k: (jnp.minimum(k, steps - 1), 0)),
            pl.BlockSpec((width, depth), lambda k: (jnp.maximum(k - steps, 0), 0)),
        ],
        out_specs=pl.BlockSpec((m, width), lambda k: (0, k)),
        out_shape=jax.ShapeDtypeStruct((m, 2 * half), jnp.bfloat16),
        compiler_params=pltpu.CompilerParams(vmem_limit_bytes=VMEM_LIMIT),
        cost_estimate=cost(4 * m * depth * half, 2 * (m * depth + 2 * half * depth + 2 * m * half)),
        name="product",
    )(a, own, other)


def leave_kernel(core_ref, prod_ref, normed_ref, gain_ref, bias_ref, w_ref, out_ref, scr):
    hidden, rows, width = prod_ref.shape
    channels = normed_ref.shape[-1]
    values = prod_ref[...].astype(jnp.float32)
    average = jnp.sum(values, axis=0, keepdims=True) * (1.0 / hidden)
    centred = values - average
    spread = jnp.sum(centred * centred, axis=0, keepdims=True) * (1.0 / hidden)
    scaled = centred * lax.rsqrt(spread + 1e-05)
    for t in range(width // LANES):
        scr[t] = scaled[:, :, t * LANES : (t + 1) * LANES].reshape(hidden * rows, LANES)
    gain = gain_ref[...]
    bias = bias_ref[...]
    for i in range(rows):
        post = jnp.concatenate(
            [
                (scr[t, pl.ds(i, hidden, stride=rows), :].T * gain + bias).astype(jnp.bfloat16)
                for t in range(width // LANES)
            ],
            axis=0,
        )
        normed = normed_ref[i].reshape(width, channels)
        result = jnp.dot(
            jnp.concatenate([post, normed], axis=1), w_ref[...], preferred_element_type=jnp.float32
        )
        update = gate_by(result[:, channels:], result[:, :channels])
        out_ref[i] = update.astype(jnp.bfloat16).reshape(out_ref.shape[1:])


def leave(core, prod, normed, gain, bias, w, width=512):
    hidden, rows, columns = prod.shape
    _, groups, _, part, channels = normed.shape
    count = width // part
    steps = groups // count
    pair_spec = pl.BlockSpec(
        (rows, count, None, part, channels),
        lambda k, c: (0, lax.rem(k, steps), jnp.where(k < steps, c[0], 1 - c[0]), 0, 0),
    )
    return pl.pallas_call(
        leave_kernel,
        grid_spec=pltpu.PrefetchScalarGridSpec(
            num_scalar_prefetch=1,
            grid=(columns // width,),
            in_specs=[
                pl.BlockSpec((hidden, rows, width), lambda k, c: (0, 0, k)),
                pair_spec,
                whole(1, hidden),
                whole(1, hidden),
                whole(*w.shape),
            ],
            out_specs=pair_spec,
            scratch_shapes=[pltpu.VMEM((width // LANES, hidden * rows, LANES), jnp.float32)],
        ),
        out_shape=jax.ShapeDtypeStruct(normed.shape, jnp.bfloat16),
        compiler_params=pltpu.CompilerParams(vmem_limit_bytes=VMEM_LIMIT),
        cost_estimate=cost(4 * prod.size * channels, 6 * prod.size, prod.size),
        name="leave",
    )(core, prod, normed, gain, bias, w)


def shards(pair, pair_mask, in_gain, in_bias, w_proj, w_gate, out_gain, out_bias, w_out):
    rows, total, channels = pair.shape
    hidden = w_out.shape[0]
    given = (pair, pair_mask, in_gain.reshape(1, -1), in_bias.reshape(1, -1), w_proj)
    (right,) = enter("enter_right", *given, 1, False)
    left, normed = enter("enter_left", *given, 0, True)
    exchange = functools.partial(lax.all_to_all, axis_name=CHIPS, split_axis=0, concat_axis=0, tiled=True)
    matrix = (hidden * rows, total)
    own = exchange(right)
    other = lax.ppermute(own, "core", [(0, 1), (1, 0)])
    prod = product(exchange(left).reshape(matrix), own.reshape(matrix), other.reshape(matrix))
    back = exchange(prod.reshape(hidden, rows, total))
    w_both = jnp.zeros((hidden + channels, 2 * channels), jnp.bfloat16)
    w_both = w_both.at[:hidden, :channels].set(w_out * 0.5).at[hidden:, channels:].set(w_gate * 0.5)
    out = leave(
        lax.axis_index("core").reshape(1),
        back,
        normed.reshape(rows, NZ * NY, NCORE, NX * rows, channels),
        out_gain.reshape(1, -1),
        out_bias.reshape(1, -1),
        w_both,
    )
    return out.reshape(pair.shape)


def solution(mesh):
    fine = Mesh(mesh.devices.reshape(NZ, NY, NCORE, NX), ("z", "y", "core", "x"))
    split = ("z", "y", "core", "x")
    return jax.shard_map(
        shards,
        mesh=fine,
        in_specs=(P(split), P(split), P(), P(), P(), P(), P(), P(), P()),
        out_specs=P(split),
        check_vma=False,
    )
```

```python
import functools

import jax
import jax.numpy as jnp
from jax import lax
from jax.experimental import pallas as pl
from jax.experimental.pallas import tpu as pltpu
from jax.sharding import Mesh
from jax.sharding import PartitionSpec as P

NZ, NY, NCORE, NX = 8, 4, 2, 4
CHIPS = ("z", "y", "x")
ROWS = 8
LANES = 128
MIB = 1024 * 1024
VMEM_LIMIT = 56 * MIB


def rows_norm(values, gain, bias):
    channels = values.shape[-1]
    share = jnp.full((channels, channels), 1.0 / channels, jnp.bfloat16)
    average = jnp.dot(values, share, preferred_element_type=jnp.float32)
    centred = values.astype(jnp.float32) - average
    spread = jnp.mean(centred * centred, axis=-1, keepdims=True)
    return centred * lax.rsqrt(spread + 1e-05) * gain + bias


def gate_by(half_gate, half_value):
    return half_value * jnp.tanh(half_gate) + half_value


def turned(w_ref, turned_ref):
    @pl.when(pl.program_id(0) == 0)
    def _():
        turned_ref[...] = (w_ref[...].astype(jnp.float32).T * 0.5).astype(jnp.bfloat16)

    return turned_ref


def gated(w_ref, normed, keep):
    hidden = w_ref.shape[0] // 2
    proj = lax.dot_general(
        w_ref[...], normed, (((1,), (1,)), ((), ())), preferred_element_type=jnp.float32
    )
    return gate_by(proj[:hidden], proj[hidden:] * keep)


def spread_rows(scr, i, value):
    for t in range(scr.shape[0]):
        part = value[:, t * LANES : (t + 1) * LANES]
        scr[t, pl.ds(i, value.shape[0], stride=ROWS), :] = part


def collect(scr, out_ref):
    hidden = out_ref.shape[0]
    for t in range(scr.shape[0]):
        block = scr[t].reshape(hidden, ROWS, LANES)
        out_ref[:, :, t * LANES : (t + 1) * LANES] = block.astype(jnp.bfloat16)


def enter_kernel(pair_ref, mask_ref, gain_ref, bias_ref, w_ref, side_ref, *refs):
    *normed_refs, scr, w_scr = refs
    weights = turned(w_ref, w_scr)
    keep = mask_ref[...].astype(jnp.float32)
    rows, width, channels = pair_ref.shape
    values = pair_ref[...].reshape(rows * width, channels)
    normed = rows_norm(values, gain_ref[...], bias_ref[...]).astype(jnp.bfloat16)
    for i in range(rows):
        part = normed[i * width : (i + 1) * width]
        for normed_ref in normed_refs:
            normed_ref[i] = part
        spread_rows(scr, i, gated(weights, part, keep[i : i + 1]))
    collect(scr, side_ref)


def whole(*shape):
    return pl.BlockSpec(shape, lambda *k: (0,) * len(shape))


def cost(flops, bytes_accessed, transcendentals=0):
    return pl.CostEstimate(
        flops=flops, bytes_accessed=bytes_accessed, transcendentals=transcendentals
    )


def enter(name, pair, mask, gain, bias, w_proj, side_at, normed_too, width=512):
    rows, total, channels = pair.shape
    hidden = w_proj.shape[1] // 4
    pair_spec = pl.BlockSpec((rows, width, channels), lambda k: (0, k, 0))
    side = jax.ShapeDtypeStruct((hidden, rows, total), jnp.bfloat16)
    return pl.pallas_call(
        enter_kernel,
        grid=(total // width,),
        in_specs=[
            pair_spec,
            pl.BlockSpec((rows, width), lambda k: (0, k)),
            whole(1, channels),
            whole(1, channels),
            pl.BlockSpec((channels, 2 * hidden), lambda k: (0, side_at)),
        ],
        out_specs=[pl.BlockSpec((hidden, rows, width), lambda k: (0, 0, k))] + [pair_spec] * normed_too,
        out_shape=[side] + [jax.ShapeDtypeStruct(pair.shape, jnp.bfloat16)] * normed_too,
        scratch_shapes=[
            pltpu.VMEM((width // LANES, hidden * rows, LANES), jnp.float32),
            pltpu.VMEM((2 * hidden, channels), jnp.bfloat16),
        ],
        compiler_params=pltpu.CompilerParams(vmem_limit_bytes=VMEM_LIMIT),
        cost_estimate=cost(4 * pair.size * hidden, 6 * pair.size, pair.size),
        name=name,
    )(pair, mask, gain, bias, w_proj)


def product_kernel(own_steps, a_ref, own_ref, other_ref, out_ref):
    def multiply(b_ref):
        out_ref[...] = lax.dot_general(
            a_ref[...],
            b_ref[...],
            (((1,), (1,)), ((), ())),
            preferred_element_type=jnp.float32,
        ).astype(jnp.bfloat16)

    step = pl.program_id(0)
    pl.when(step < own_steps)(lambda: multiply(own_ref))
    pl.when(step >= own_steps)(lambda: multiply(other_ref))


def product(a, own, other, width=512):
    m, depth = a.shape
    half = own.shape[0]
    steps = half // width
    return pl.pallas_call(
        functools.partial(product_kernel, steps),
        grid=(2 * steps,),
        in_specs=[
            whole(m, depth),
            pl.BlockSpec((width, depth), lambda k: (jnp.minimum(k, steps - 1), 0)),
            pl.BlockSpec((width, depth), lambda k: (jnp.maximum(k - steps, 0), 0)),
        ],
        out_specs=pl.BlockSpec((m, width), lambda k: (0, k)),
        out_shape=jax.ShapeDtypeStruct((m, 2 * half), jnp.bfloat16),
        compiler_params=pltpu.CompilerParams(vmem_limit_bytes=VMEM_LIMIT),
        cost_estimate=cost(4 * m * depth * half, 2 * (m * depth + 2 * half * depth + 2 * m * half)),
        name="product",
    )(a, own, other)


def leave_kernel(core_ref, prod_ref, normed_ref, gain_ref, bias_ref, w_ref, out_ref, scr):
    hidden, rows, width = prod_ref.shape
    channels = normed_ref.shape[-1]
    values = prod_ref[...].astype(jnp.float32)
    average = jnp.sum(values, axis=0, keepdims=True) * (1.0 / hidden)
    centred = values - average
    spread = jnp.sum(centred * centred, axis=0, keepdims=True) * (1.0 / hidden)
    scaled = centred * lax.rsqrt(spread + 1e-05)
    for t in range(width // LANES):
        scr[t] = scaled[:, :, t * LANES : (t + 1) * LANES].reshape(hidden * rows, LANES)
    gain = gain_ref[...]
    bias = bias_ref[...]
    for i in range(rows):
        post = jnp.concatenate(
            [
                (scr[t, pl.ds(i, hidden, stride=rows), :].T * gain + bias).astype(jnp.bfloat16)
                for t in range(width // LANES)
            ],
            axis=0,
        )
        normed = normed_ref[i].reshape(width, channels)
        result = jnp.dot(
            jnp.concatenate([post, normed], axis=1), w_ref[...], preferred_element_type=jnp.float32
        )
        update = gate_by(result[:, channels:], result[:, :channels])
        out_ref[i] = update.astype(jnp.bfloat16).reshape(out_ref.shape[1:])


def leave(core, prod, normed, gain, bias, w, width=512):
    hidden, rows, columns = prod.shape
    _, groups, _, part, channels = normed.shape
    count = width // part
    steps = groups // count
    pair_spec = pl.BlockSpec(
        (rows, count, None, part, channels),
        lambda k, c: (0, lax.rem(k, steps), jnp.where(k < steps, c[0], 1 - c[0]), 0, 0),
    )
    return pl.pallas_call(
        leave_kernel,
        grid_spec=pltpu.PrefetchScalarGridSpec(
            num_scalar_prefetch=1,
            grid=(columns // width,),
            in_specs=[
                pl.BlockSpec((hidden, rows, width), lambda k, c: (0, 0, k)),
                pair_spec,
                whole(1, hidden),
                whole(1, hidden),
                whole(*w.shape),
            ],
            out_specs=pair_spec,
            scratch_shapes=[pltpu.VMEM((width // LANES, hidden * rows, LANES), jnp.float32)],
        ),
        out_shape=jax.ShapeDtypeStruct(normed.shape, jnp.bfloat16),
        compiler_params=pltpu.CompilerParams(vmem_limit_bytes=VMEM_LIMIT),
        cost_estimate=cost(4 * prod.size * channels, 6 * prod.size, prod.size),
        name="leave",
    )(core, prod, normed, gain, bias, w)


def shards(pair, pair_mask, in_gain, in_bias, w_proj, w_gate, out_gain, out_bias, w_out):
    rows, total, channels = pair.shape
    hidden = w_out.shape[0]
    given = (pair, pair_mask, in_gain.reshape(1, -1), in_bias.reshape(1, -1), w_proj)
    (right,) = enter("enter_right", *given, 1, False)
    left, normed = enter("enter_left", *given, 0, True)
    exchange = functools.partial(lax.all_to_all, axis_name=CHIPS, split_axis=0, concat_axis=0, tiled=True)
    matrix = (hidden * rows, total)
    own = exchange(right)
    other = lax.ppermute(own, "core", [(0, 1), (1, 0)])
    prod = product(exchange(left).reshape(matrix), own.reshape(matrix), other.reshape(matrix))
    back = exchange(prod.reshape(hidden, rows, total))
    w_both = jnp.zeros((hidden + channels, 2 * channels), jnp.bfloat16)
    w_both = w_both.at[:hidden, :channels].set(w_out * 0.5).at[hidden:, channels:].set(w_gate * 0.5)
    out = leave(
        lax.axis_index("core").reshape(1),
        back,
        normed.reshape(rows, NZ * NY, NCORE, NX * rows, channels),
        out_gain.reshape(1, -1),
        out_bias.reshape(1, -1),
        w_both,
    )
    return out.reshape(pair.shape)


def solution(mesh):
    fine = Mesh(mesh.devices.reshape(NZ, NY, NCORE, NX), ("z", "y", "core", "x"))
    split = ("z", "y", "core", "x")
    return jax.shard_map(
        shards,
        mesh=fine,
        in_specs=(P(split), P(split), P(), P(), P(), P(), P(), P(), P()),
        out_specs=P(split),
        check_vma=False,
    )
```
